32 devices in a mesh: grp: 4 (over y, x), slab: 8 (over z, core).
Axes of the slice: x: 2, y: 2, z: 4, core: 2. Of those that a mesh axis runs over, the one named last changes fastest.
Arguments:
- source: float32 [128, 32, 1024], P('grp', None, 'slab'), may hold values from -6 to 6
- occupancy: int32 [16, 4, 128], P('grp', None, 'slab'), may hold values 0 or 1
- classes: int32 [16, 4, 128], P('grp', None, 'slab'), may hold values from 0 to 15
- screen_table: float32 [16], replicated, may hold values from 0.5 to 8
- parents: int32 [8, 2, 64], P('grp', None, 'slab'), may hold values from 0 to 31, as said below
- coarse: float32 [4, 32, 512], P('grp', 'slab'), may hold values from -6 to 6
Outputs:
- middle_field: float32 [64, 16, 512], P('grp', None, 'slab')
- finest_field: float32 [128, 32, 1024], P('grp', None, 'slab')
The draws below stay inside these ranges and needn't reach their ends.
Inputs may be any that keep to these rules, and one draw needn't show every extreme that they name: parents[I, J, K] is the position, in the list of the group that holds the brick, of the depth-12 brick containing depth-13 brick (I, J, K); each group's list holds each depth-12 brick of the group's region once, so each position is the parent of eight depth-13 bricks. The parent of a brick on slab index s lies in list positions [(s - 1) * 4, (s + 2) * 4).
All inputs are finite; a program needn't handle non-finite values. No bound on the sum of `occupancy` on one device may be relied on, other than what follows from the above.
Results may differ from the reference program's by a relative error of at most 0.00002.
Values sent between devices are 32-bit elements; how exact they have to be, the bound alone decides.
A program may use at most 128 MiB of HBM per device.

```python
import math
import jax
import jax.numpy as jnp
from jax import lax

BRICK = 8
SWEEPS = 3
CLASSES = 16
CX = 32
NY = 32
CZ = 128
NX = 128
NZ = 1024
LIST = 32
N_GRP = 4
N_SLAB = 8


def draw_parents(key, part):
    groups_x = CX // (4 * BRICK)
    groups_y = NY // (4 * BRICK)
    groups_z = CZ // (4 * BRICK)
    shard_len = groups_x * groups_y * groups_z
    total = shard_len * N_SLAB

    def one_group(group_key):
        first_key, second_key = jax.random.split(group_key)
        offset = jax.random.randint(first_key, (), 1, shard_len, dtype=jnp.int32)
        indices = jnp.arange(total, dtype=jnp.int32)
        segment = (indices - offset + shard_len) // shard_len
        shuffle = jax.random.permutation(second_key, total).astype(jnp.int32)
        placed = jnp.argsort(segment * total + shuffle, stable=True)
        return placed.astype(jnp.int32)
    keys = jax.random.split(jax.random.fold_in(key, 11), N_GRP)
    placement = jax.vmap(one_group)(keys)
    count_x = NX // (2 * BRICK)
    count_y = NY // (2 * BRICK)
    count_z = NZ // (2 * BRICK)
    index_x = jnp.arange(count_x, dtype=jnp.int32)[:, None, None]
    index_y = jnp.arange(count_y, dtype=jnp.int32)[None, :, None]
    index_z = jnp.arange(count_z, dtype=jnp.int32)[None, None, :]
    group = index_x // (CX // (2 * BRICK))
    within_x = index_x % (CX // (2 * BRICK)) // 2
    coarse_y = index_y // 2
    coarse_z = index_z // 2
    slab_index = coarse_z // groups_z
    within_z = coarse_z % groups_z
    geometric = ((slab_index * groups_x + within_x) * groups_y + coarse_y) * groups_z + within_z
    group_full = jnp.broadcast_to(group, (count_x, count_y, count_z))
    geometric_full = jnp.broadcast_to(geometric, (count_x, count_y, count_z))
    return placement[group_full, geometric_full].astype(jnp.int32)


def plant(values, stream_key, least, largest):
    shape = values.shape
    index_at = [jax.random.randint(jax.random.fold_in(stream_key, axis), (), 0, shape[axis]) for axis in range(len(shape))]
    values = values.at[tuple(index_at)].set(least)
    longest = shape.index(max(shape))
    index_at[longest] = (index_at[longest] + 1) % shape[longest]
    return values.at[tuple(index_at)].set(largest)


def level_of(own_key, dims, cuts, low, high):
    def one(dim, blocks):
        heights = jax.random.uniform(jax.random.fold_in(jax.random.fold_in(own_key, 6), dim), (blocks,), jnp.float32, low / len(cuts), high / len(cuts))
        return jnp.repeat(jnp.exp(heights), dims[dim] // blocks).reshape((-1,) + (1,) * (len(dims) - dim - 1))

    factor_of = one(*cuts[0])
    for cut in cuts[1:]:
        factor_of = factor_of * one(*cut)
    return factor_of


def gaussian(rng, dims, scale, most, shards=(), held_as=jnp.bfloat16):
    entries = scale * jax.random.normal(rng, dims, jnp.float32)
    if shards:
        entries = entries * level_of(rng, dims, shards, -0.22, 0.18)
    return jnp.clip(entries, -most, most).astype(held_as)


def setup_inputs(seed: int = 0) -> dict:
    arg_keys = jax.random.split(jax.random.key(seed), 7)
    return {
        "source": gaussian(arg_keys[0], (NX, NY, NZ), 1.0, 6.0, ((0, 4), (2, 8)), jnp.float32),
        "occupancy": plant((jax.random.randint(arg_keys[1], (NX // BRICK, NY // BRICK, NZ // BRICK), 0, 4) < 3).astype(jnp.int32), jax.random.fold_in(arg_keys[1], 1), 0, 1),
        "classes": plant(jax.random.randint(arg_keys[2], (NX // BRICK, NY // BRICK, NZ // BRICK), 0, CLASSES), jax.random.fold_in(arg_keys[2], 1), 0, CLASSES - 1).astype(jnp.int32),
        "screen_table": jnp.clip(jnp.exp(jax.random.uniform(arg_keys[3], (CLASSES,), jnp.float32, math.log(0.5), math.log(8.0))), 0.5, 8.0),
        "parents": draw_parents(jax.random.fold_in(arg_keys[6], 71), 0),
        "coarse": gaussian(arg_keys[5], (N_GRP, LIST, BRICK ** 3), 1.0, 6.0, ((0, 4), (1, 8)), jnp.float32),
    }


screen_strength = 4.0
relaxation = 2.0 / 3.0
stiff_diagonal = 8.0 / 3.0
mass_diagonal = 8.0 / 27.0


def expand(values, factor):
    first, second, third = values.shape
    wide = jnp.broadcast_to(values[:, None, :, None, :, None], (first, factor, second, factor, third, factor))
    return wide.reshape(first * factor, second * factor, third * factor)


def mass_along(values, along):
    length = values.shape[along]
    lower = lax.slice_in_dim(values, 0, length - 2, axis=along)
    middle = lax.slice_in_dim(values, 1, length - 1, axis=along)
    upper = lax.slice_in_dim(values, 2, length, axis=along)
    return (lower + 4.0 * middle + upper) / 6.0


def stiff_along(values, along):
    length = values.shape[along]
    lower = lax.slice_in_dim(values, 0, length - 2, axis=along)
    middle = lax.slice_in_dim(values, 1, length - 1, axis=along)
    upper = lax.slice_in_dim(values, 2, length, axis=along)
    return 2.0 * middle - lower - upper


def relax_step(padded, source, inverse, screen):
    padded_all = jnp.pad(padded, ((0, 0), (1, 1), (0, 0)))
    mass_z = mass_along(padded_all, 2)
    stiff_z = stiff_along(padded_all, 2)
    mass_yz = mass_along(mass_z, 1)
    mixed = stiff_along(mass_z, 1) + mass_along(stiff_z, 1)
    laplace = stiff_along(mass_yz, 0) + mass_along(mixed, 0)
    mass_all = mass_along(mass_yz, 0)
    center = padded[1:-1, :, 1:-1]
    return center + relaxation * inverse * (source - laplace - screen * mass_all)


def sweep_level(field, source, screen_brick, inverse_brick, spread, extent):
    padded = jnp.pad(field, ((1, 1), (0, 0), (1, 1)))
    bricks = extent // spread

    def one_group(column):
        part = lax.dynamic_slice_in_dim(padded, column * extent, extent + 2, 0)
        right = lax.dynamic_slice_in_dim(source, column * extent, extent, 0)
        screen = expand(lax.dynamic_slice_in_dim(screen_brick, column * bricks, bricks, 0), spread)
        inverse = expand(lax.dynamic_slice_in_dim(inverse_brick, column * bricks, bricks, 0), spread)
        return relax_step(part, right, inverse, screen)

    result = lax.map(one_group, jnp.arange(N_GRP, dtype=jnp.int32))
    return result.reshape(field.shape)


def lift(brick_rows, count_x, count_y, count_z):
    half = BRICK // 2
    cells = brick_rows.reshape(count_x, count_y, count_z, 2, half, 2, half, 2, half)
    pairs = jnp.arange(2, dtype=jnp.int32)
    pick_x = ((jnp.arange(count_x, dtype=jnp.int32) % 2)[:, None] == pairs).astype(jnp.float32)
    pick_y = ((jnp.arange(count_y, dtype=jnp.int32) % 2)[:, None] == pairs).astype(jnp.float32)
    pick_z = ((jnp.arange(count_z, dtype=jnp.int32) % 2)[:, None] == pairs).astype(jnp.float32)
    chosen = jnp.sum(cells * pick_x[:, None, None, :, None, None, None, None, None], axis=3)
    chosen = jnp.sum(chosen * pick_y[None, :, None, None, :, None, None, None], axis=4)
    chosen = jnp.sum(chosen * pick_z[None, None, :, None, None, :, None], axis=5)
    fine = jnp.broadcast_to(chosen[:, :, :, :, None, :, None, :, None], (count_x, count_y, count_z, half, 2, half, 2, half, 2))
    fine = fine.reshape(count_x, count_y, count_z, BRICK, BRICK, BRICK)
    return fine.transpose(0, 3, 1, 4, 2, 5).reshape(count_x * BRICK, count_y * BRICK, count_z * BRICK)


def reference(source, occupancy, classes, screen_table, parents, coarse):
    occupied = occupancy.astype(jnp.float32)
    labels = jnp.arange(CLASSES, dtype=jnp.int32)
    weight = jnp.sum(jnp.where(classes[..., None] == labels, screen_table, 0.0), axis=-1)
    screen_brick = screen_strength * weight
    inverse_brick = occupied / (stiff_diagonal + screen_brick * mass_diagonal)
    count_x, count_y, count_z = parents.shape
    group = jnp.arange(count_x, dtype=jnp.int32) // (CX // (2 * BRICK))
    flat = coarse.reshape(N_GRP * LIST, BRICK ** 3)
    position = (group[:, None, None] * LIST + parents).reshape(-1)
    brick_rows = jnp.take(flat, position, axis=0)
    middle_field = lift(brick_rows, count_x, count_y, count_z) * expand(occupied, BRICK // 2)
    size_x, size_y, size_z = source.shape
    source_mid = 0.25 * source.reshape(size_x // 2, 2, size_y // 2, 2, size_z // 2, 2).sum(axis=(1, 3, 5))
    for sweep_index in range(SWEEPS):
        middle_field = sweep_level(middle_field, source_mid, screen_brick, inverse_brick, BRICK // 2, CX // 2)
    finest_field = expand(middle_field, 2) * expand(occupied, BRICK)
    for sweep_index in range(SWEEPS):
        finest_field = sweep_level(finest_field, source, screen_brick, inverse_brick, BRICK, CX)
    return middle_field, finest_field
```

```python
import functools
import jax
import jax.numpy as jnp
import numpy as np
from jax import lax
from jax.experimental import pallas as pl
from jax.experimental.pallas import tpu as pltpu
from jax.sharding import PartitionSpec as P

BRICK = 8
F32 = jnp.float32
BF16 = jnp.bfloat16
MESH = pl.DeviceIdType.MESH
VM = pl.BlockSpec(memory_space=pltpu.VMEM)
SM = pl.BlockSpec(memory_space=pltpu.SMEM)

NEAR = [(dx, dz) for dx in (-1, 0, 1) for dz in (-2, -1, 0, 1, 2) if (dx, dz) != (0, 0)]


def split3(a):
    hi = a.astype(BF16)
    rest = a - hi.astype(F32)
    mid = rest.astype(BF16)
    lo = (rest - mid.astype(F32)).astype(BF16)
    return hi, mid, lo


def dot3(a, b):
    parts = [jnp.dot(p, b, preferred_element_type=F32) for p in split3(a)]
    return parts[0] + (parts[1] + parts[2])


def iota(shape, dim):
    return lax.broadcasted_iota(jnp.int32, shape, dim)


def exchange_kernel(
    groups, slabs, source, occ, cls, par, coarse, fold,
    msgz, s13, rz, rc, rf, rfx, rsrc, rs13,
    msgx, xs13, send_sem, recv_sem,
):
    g = lax.axis_index("grp")
    s = lax.axis_index("slab")
    nx, ny, nz = source.shape
    half = nx // 2

    def exists(dx, dz):
        return (g + dx >= 0) & (g + dx < groups) & (s + dz >= 0) & (s + dz < slabs)

    for ref in (rz, rc, rf, rfx, rsrc, rs13):
        ref[...] = jnp.zeros(ref.shape, F32)
    barrier = pltpu.get_barrier_semaphore()
    count = jnp.int32(0)
    for dx, dz in NEAR:
        here = exists(dx, dz)
        count = count + here.astype(jnp.int32)

        @pl.when(here)
        def _():
            pl.semaphore_signal(
                barrier, inc=1, device_id={"grp": g + dx, "slab": s + dz}, device_id_type=MESH
            )

    lane = iota((8, 128), 1)
    for c in range(4):
        msgz[4 * c : 4 * c + 4, :] = coarse[0, :, 128 * c : 128 * c + 128]
    msgz[16:32, :] = jnp.zeros((16, 128), F32)
    bx = occ.shape[0]
    for i in range(bx):
        msgz[16 + 4 * i : 20 + 4 * i, 0:16] = occ[i].astype(F32)
        msgz[16 + 4 * i : 20 + 4 * i, 16:32] = cls[i].astype(F32)
    msgz[16:32, 32:40] = jnp.broadcast_to(par[0, 0:1, :].astype(F32), (16, 8))
    for t in range(4):
        tile = jnp.zeros((8, 128), F32)
        for j in range(8):
            for yh in range(4):
                off = (j * 4 + yh) * 4
                v = source[t * 8 + j, yh * 8 : yh * 8 + 8, :]
                r = pltpu.roll(v, off, 1) if off else v
                tile = jnp.where(((lane + 2 - off) & 127) < 4, r, tile)
        msgz[32 + 8 * t : 40 + 8 * t, :] = tile
    for m in range(half):
        a = source[2 * m, pl.ds(0, 16, 2), :] + source[2 * m, pl.ds(1, 16, 2), :]
        b = source[2 * m + 1, pl.ds(0, 16, 2), :] + source[2 * m + 1, pl.ds(1, 16, 2), :]
        s13[m] = a + b
    flat = s13[...].reshape(half * 16, 128)
    s13[...] = dot3(flat, fold[...]).reshape(half, 16, 128)
    for t in range(2):
        tile = jnp.zeros((8, 128), F32)
        for j in range(8):
            for yh in range(2):
                off = (j * 2 + yh) * 8
                v = s13[t * 8 + j, yh * 8 : yh * 8 + 8, :]
                low = pltpu.roll(v, (off + 4) % 128, 1)
                high = pltpu.roll(v, (off + 68) % 128, 1)
                tile = jnp.where((lane >= off) & (lane < off + 4), high, tile)
                tile = jnp.where((lane >= off + 4) & (lane < off + 8), low, tile)
        msgz[64 + 8 * t : 72 + 8 * t, :] = tile
    lane16 = iota((16, 128), 1)
    for side in range(2):
        msgx[side, 0:8, :] = msgz[8 * side : 8 * side + 8, :]
        msgx[side, 8:16, :] = msgz[16 + 8 * side : 24 + 8 * side, :]
        msgx[side, 16:24, :] = msgz[32 + 24 * side : 40 + 24 * side, :]
        msgx[side, 24:32, :] = msgz[64 + 8 * side : 72 + 8 * side, :]
        base = (half - 4) * side
        for i in range(2):
            xs13[side, i] = jnp.where(
                lane16 < 64, s13[base + i], pltpu.roll(s13[base + 2 + i], 64, 1)
            )

    pl.semaphore_wait(barrier, count)

    copies = []

    def add(src, dst, dx, dz):
        k = len(copies)
        copies.append((src, dst, dx, dz, k))

    for dz in (-1, 1):
        add(msgz, rz.at[(1 - dz) // 2], 0, dz)
    for dx in (-1, 1):
        side, slot = (dx + 1) // 2, (1 - dx) // 2
        add(source.at[(nx - 2) * side : (nx - 2) * side + 2], rsrc.at[slot], dx, 0)
        add(xs13.at[side], rs13.at[slot], dx, 0)
        add(msgx.at[side, 0:16], rc.at[slot, 1, 0:16], dx, 0)
        for dz in (-1, 1):
            add(msgx.at[side], rc.at[slot, 1 - dz], dx, dz)
        for dz in (-2, 2):
            add(msgx.at[side, 0:8], rfx.at[slot, (2 - dz) // 4], dx, dz)
    for dz in (-2, 2):
        add(msgz.at[0:16], rf.at[(2 - dz) // 4], 0, dz)

    made = []
    for src, dst, dx, dz, k in copies:
        copy = pltpu.make_async_remote_copy(
            src_ref=src, dst_ref=dst, send_sem=send_sem.at[k], recv_sem=recv_sem.at[k],
            device_id={"grp": g + dx, "slab": s + dz}, device_id_type=MESH,
        )
        made.append((copy, dx, dz))
        pl.when(exists(dx, dz))(copy.start)
    for copy, dx, dz in made:
        pl.when(exists(-dx, -dz))(copy.wait_recv)
    for copy, dx, dz in made:
        pl.when(exists(dx, dz))(copy.wait_send)


def y_sum(v):
    rows = v.shape[0]
    at = iota(v.shape, 0)
    up = jnp.where(at == 0, 0.0, pltpu.roll(v, 1, 0))
    down = jnp.where(at == rows - 1, 0.0, pltpu.roll(v, rows - 1, 0))
    return up + down


def parts_of(v, zs):
    b = 4.0 * v + zs
    a = 4.0 * v + y_sum(v)
    c = 4.0 * b + y_sum(b)
    return c, a + b


def smooth_kernel(
    slab_rows, table, source, msgz, s13, rz, rc, rf, rfx, rsrc, rs13, fc, fd, fe,
    middle, finest,
    pf, px, qx, pm, qm, occm, occf, v13, wr13, v14, wr14,
):
    s = lax.axis_index("slab")
    nx, ny, nz = source.shape
    half = nx // 2

    def ext(own, low, high):
        lane = iota(own.shape, 1)
        return jnp.where(
            lane < 40, own, jnp.where(lane < 80, pltpu.roll(low, 40, 1), pltpu.roll(high, 80, 1))
        )

    e_low = ext(rc[0, 1, 8:16], rc[0, 0, 8:16], rc[0, 2, 8:16])
    e_own = ext(msgz[16:32], rz[0, 16:32], rz[1, 16:32])
    e_high = ext(rc[1, 1, 8:16], rc[1, 0, 8:16], rc[1, 2, 8:16])
    e_all = jnp.concatenate([e_low, e_own, e_high], axis=0)
    spread = jnp.dot(e_all.astype(BF16), fc[...], preferred_element_type=F32)

    def coefficients(occupied, label):
        weight = jnp.zeros_like(label)
        for i in range(table.shape[0]):
            weight = jnp.where(label == float(i), table[i], weight)
        screen = 4.0 * weight
        inverse = occupied / (8.0 / 3.0 + screen * (8.0 / 27.0))
        p = inverse * (1.0 / 9.0)
        return p, p * ((screen - 18.0) * (1.0 / 36.0))

    of, om = spread[:, 0:256], spread[:, 512:640]
    p, q = coefficients(of, spread[:, 256:512])
    pf[...] = p
    for i in range(8):
        for j in range(4):
            for tile in range(2):
                cut = slice(128 * tile, 128 * tile + 128)
                one = slice(4 * i + j, 4 * i + j + 1)
                px[i, tile, 8 * j : 8 * j + 8, :] = jnp.broadcast_to(p[one, cut], (8, 128))
                qx[i, tile, 8 * j : 8 * j + 8, :] = jnp.broadcast_to(q[one, cut], (8, 128))
    p, q = coefficients(om, spread[:, 640:768])
    for i in range(8):
        for value, ref in ((p, pm), (q, qm), (om, occm), (of, occf)):
            rows = [
                jnp.broadcast_to(value[4 * i + j : 4 * i + j + 1], (4, value.shape[1]))
                for j in range(4)
            ]
            ref[i] = jnp.concatenate(rows, axis=0)

    base = ((s - 2) * slab_rows).astype(F32)

    def bricks(ext_rows, blocks, cs):
        cand = jnp.concatenate(blocks, axis=0)
        n_rows, n_cand = cs * 8, 5 * cs * 4
        row = jnp.broadcast_to(ext_rows[0:1], (n_rows, 128))
        kk = iota((n_rows, 128), 0) & 7
        at = jnp.where(kk == 0, 78, jnp.where(kk == 5, 112, 30 + 2 * kk))
        at = jnp.where(kk > 5, 127, at)
        pos = jnp.sum(jnp.where(iota((n_rows, 128), 1) == at, row, 0.0), axis=1, keepdims=True)
        col = iota((n_rows, n_cand), 1)
        r = iota((n_rows, n_cand), 0)
        block = col // (cs * 4)
        c_of = (col // 4) % cs
        place = (block * 4 + col % 4).astype(F32)
        hot = ((c_of == r // 8) & (pos - base == place)).astype(F32).astype(BF16)
        hi, mid, lo = split3(cand)
        return [jnp.dot(hot, part, preferred_element_type=F32) for part in (hi, mid, lo)]

    own = bricks(e_own, [rf[0], rz[0, 0:16], msgz[0:16], rz[1, 0:16], rf[1]], 4)
    sides = [
        bricks(e, [rfx[i, 0], rc[i, 0, 0:8], rc[i, 1, 0:8], rc[i, 2, 0:8], rfx[i, 1]], 2)
        for i, e in ((0, e_low), (1, e_high))
    ]
    keep = (iota((16, 128), 1) // 8) == iota((16, 128), 0)
    total = None
    for part in range(3):
        lines = []
        for rows, cs in ((sides[0][part], 2), (own[part], 4), (sides[1][part], 2)):
            for c in range(cs):
                lines.append(jnp.concatenate(
                    [
                        jnp.where(keep, jnp.broadcast_to(rows[8 * c + k : 8 * c + k + 1], (16, 128)), 0.0)
                        for k in range(6)
                    ], axis=1))
        left = jnp.concatenate(lines, axis=0).astype(BF16)
        term = jnp.dot(left, fd[...], preferred_element_type=F32)
        total = term if total is None else total + term
    for i in range(1, 15):
        line = total[8 * i : 8 * i + 8]
        for a in range(2):
            plane = 2 * i - 2 + a
            v13[0, plane, pl.ds(0, 8, 2), :] = line
            v13[0, plane, pl.ds(1, 8, 2), :] = line
    for plane in range(28):
        brick = min(max((plane - 6) // 4 + 2, 0), 7)
        v13[0, plane] = v13[0, plane] * occm[brick]

    lane16 = iota((16, 128), 1)
    lane8 = iota((8, 128), 1)

    def strip13(low, high, j, own_plane):
        both = jnp.where((lane8 & 7) < 4, low, high)
        rows = []
        for yh in range(2):
            off = (j * 2 + yh) * 8
            to_low = pltpu.roll(both, (124 - off) % 128, 1)
            to_high = pltpu.roll(both, (60 - off) % 128, 1)
            rows.append(jnp.where(
                lane8 < 64, own_plane[8 * yh : 8 * yh + 8],
                jnp.where(lane8 < 96, to_high, to_low)))
        return jnp.concatenate(rows, axis=0)

    for m in range(-4, half + 4):
        if m < 0 or m >= half:
            side, i = (0, m + 4) if m < 0 else (1, m - half)
            own_plane = rs13[side, i % 2]
            if i >= 2:
                own_plane = pltpu.roll(own_plane, 64, 1)
            j = (m if m >= 0 else half + m) % 8
            plane = strip13(rc[side, 0, 24:32], rc[side, 2, 24:32], j, own_plane)
        else:
            t = m // 8
            plane = strip13(rz[0, 64 + 8 * t : 72 + 8 * t], rz[1, 64 + 8 * t : 72 + 8 * t], m % 8, s13[m])
        wr13[m + 4] = plane * (6.0 * pm[m // 4 + 2])

    def strip14(low, high, j):
        both = jnp.where((lane8 & 3) < 2, high, low)
        rows = []
        for yh in range(4):
            off = (j * 4 + yh) * 4
            rows.append(pltpu.roll(both, 128 - off, 1) if off else both)
        return rows

    for x in range(-2, nx + 2):
        if x < 0 or x >= nx:
            side, i = (0, x + 2) if x < 0 else (1, x - nx)
            own_plane = rsrc[side, i]
            j = (x if x >= 0 else nx + x) % 8
            rows = strip14(rc[side, 0, 16:24], rc[side, 2, 16:24], j)
        else:
            t = x // 8
            own_plane = source[x]
            rows = strip14(rz[0, 32 + 8 * t : 40 + 8 * t], rz[1, 32 + 8 * t : 40 + 8 * t], x % 8)
        xb = x // 8 + 2
        for yh in range(4):
            w = 6.0 * pf[4 * xb + yh : 4 * xb + yh + 1, :]
            wr14[x + 2, 8 * yh : 8 * yh + 8, 0:128] = own_plane[8 * yh : 8 * yh + 8] * w[:, 0:128]
            wr14[x + 2, 8 * yh : 8 * yh + 8, 128:256] = rows[yh] * w[:, 128:256]

    for sweep in range(3):
        old, new = sweep % 2, (sweep + 1) % 2
        first, last = sweep - 4, half + 3 - sweep

        def pieces(i):
            v = v13[old, i + 6]
            return parts_of(v, pltpu.roll(v, 1, 1) + pltpu.roll(v, 127, 1))

        c0, e0 = pieces(first - 1)
        c1, e1 = pieces(first)
        for m in range(first, last + 1):
            c2, e2 = pieces(m + 1)
            b = m // 4 + 2
            bx_e = 4.0 * e1 + (e0 + e2)
            bx_c = 4.0 * c1 + (c0 + c2)
            out = v13[old, m + 6] + wr13[m + 4] - pm[b] * (c1 + bx_e) - qm[b] * bx_c
            v13[new, m + 6] = out
            if sweep == 2 and 0 <= m < half:
                middle[m] = out[:, 0:64]
            c0, e0, c1, e1 = c1, e1, c2, e2

    wide = dot3(v13[1, 4 : half + 8].reshape((half + 4) * 16, 128), fe[...])
    for i in range(half + 4):
        m = i - 2
        line = wide[16 * i : 16 * i + 16] * occf[m // 4 + 2]
        for a in range(2):
            for b in range(2):
                v14[0, 2 * i + a, b, pl.ds(0, 16, 2), :] = line[:, 128 * b : 128 * b + 128]
                v14[0, 2 * i + a, b, pl.ds(1, 16, 2), :] = line[:, 128 * b : 128 * b + 128]

    lane32 = iota((ny, 128), 1)
    for sweep in range(3):
        old, new = sweep % 2, (sweep + 1) % 2
        first, last = sweep - 2, nx + 1 - sweep
        tiles = 2 if sweep < 2 else 1

        def pieces(i):
            v0 = v14[old, i, 0]
            v1 = v14[old, i, 1]
            l0, l1 = pltpu.roll(v0, 1, 1), pltpu.roll(v1, 1, 1)
            r0, r1 = pltpu.roll(v0, 127, 1), pltpu.roll(v1, 127, 1)
            z0 = jnp.where(lane32 == 0, l1, l0) + jnp.where(lane32 == 127, r1, r0)
            got = [parts_of(v0, z0)]
            if tiles == 2:
                z1 = jnp.where(lane32 == 0, l0, l1) + jnp.where(lane32 == 127, r0, r1)
                got.append(parts_of(v1, z1))
            return got

        def step(i, carry):
            before, now = carry
            after = pieces(i + 1)
            xb = (i + 12) // 8
            for t in range(tiles):
                cut = slice(128 * t, 128 * t + 128)
                (c0, e0), (c1, e1), (c2, e2) = before[t], now[t], after[t]
                u = c1 + (4.0 * e1 + (e0 + e2))
                w = 4.0 * c1 + (c0 + c2)
                for yh in range(4):
                    r = slice(8 * yh, 8 * yh + 8)
                    p = px[xb, t, r]
                    q = qx[xb, t, r]
                    out = v14[old, i, t, r] + wr14[i - 2, r, cut] - p * u[r] - q * w[r]
                    if sweep == 2:
                        finest[i - 4, r, :] = out
                    else:
                        v14[new, i, t, r] = out
            return now, after

        lax.fori_loop(first + 4, last + 5, step, (pieces(first + 3), pieces(first + 4)))


def constants():
    fc = np.zeros((128, 768), np.float32)
    for j in range(256):
        z = j if j < 192 else j - 256
        if 0 <= z < 128:
            at = z // 8
        elif -16 <= z < 0:
            at = 56 + z // 8
        elif 128 <= z < 144:
            at = 80 + (z - 128) // 8
        else:
            continue
        fc[at, j] = 1
        fc[at + 16, 256 + j] = 1
    for j in range(128):
        z = j if j < 96 else j - 128
        if 0 <= z < 64:
            at = z // 4
        elif -8 <= z < 0:
            at = 56 + z // 4
        elif 64 <= z < 72:
            at = 80 + (z - 64) // 4
        else:
            continue
        fc[at, 512 + j] = 1
        fc[at + 16, 640 + j] = 1
    fd = np.zeros((768, 128), np.float32)
    for k in range(6):
        for l in range(128):
            for b in range(2):
                z = (k - 1) * 16 + 2 * (l % 8) + b
                if -8 <= z < 72:
                    fd[k * 128 + l, z % 128] = 1
    fe = np.zeros((128, 256), np.float32)
    for j in range(256):
        z = j if j < 192 else j - 256
        if -8 <= z < 136:
            fe[(z // 2) % 128, j] = 1
    fold = np.zeros((128, 128), np.float32)
    for z in range(128):
        fold[z, z // 2] = 0.25
    return [jnp.asarray(a, BF16) for a in (fold, fc, fd, fe)]


def local(groups, slabs, source, occupancy, classes, screen_table, parents, coarse):
    nx, ny, nz = source.shape
    half = nx // 2
    fold, fc, fd, fe = constants()
    shape = lambda *dims: jax.ShapeDtypeStruct(dims, F32)
    moved = pl.pallas_call(
        functools.partial(exchange_kernel, groups, slabs),
        out_shape=[
            shape(80, 128), shape(half, 16, 128), shape(2, 80, 128), shape(2, 3, 32, 128),
            shape(2, 16, 128), shape(2, 2, 8, 128), shape(2, 2, ny, nz), shape(2, 2, 16, 128),
        ],
        in_specs=[VM] * 6,
        out_specs=[VM] * 8,
        scratch_shapes=[
            pltpu.VMEM((2, 32, 128), F32),
            pltpu.VMEM((2, 2, 16, 128), F32),
            pltpu.SemaphoreType.DMA((18,)),
            pltpu.SemaphoreType.DMA((18,)),
        ],
        compiler_params=pltpu.CompilerParams(
            collective_id=0, has_side_effects=True, vmem_limit_bytes=24 << 20
        ),
        name="exchange",
    )(source, occupancy, classes, parents, coarse, fold)
    return pl.pallas_call(
        functools.partial(smooth_kernel, coarse.shape[1]),
        out_shape=[shape(half, ny // 2, nz // 2), shape(nx, ny, nz)],
        in_specs=[SM] + [VM] * 12,
        out_specs=[VM] * 2,
        scratch_shapes=[
            pltpu.VMEM((32, 256), F32),
            pltpu.VMEM((8, 2, ny, 128), F32), pltpu.VMEM((8, 2, ny, 128), F32),
            pltpu.VMEM((8, 16, 128), F32), pltpu.VMEM((8, 16, 128), F32),
            pltpu.VMEM((8, 16, 128), F32), pltpu.VMEM((8, 16, 256), F32),
            pltpu.VMEM((2, half + 12, 16, 128), F32),
            pltpu.VMEM((half + 8, 16, 128), F32),
            pltpu.VMEM((2, nx + 8, 2, ny, 128), F32),
            pltpu.VMEM((nx + 4, ny, 256), F32),
        ],
        compiler_params=pltpu.CompilerParams(vmem_limit_bytes=32 << 20),
        name="smooth",
    )(screen_table, source, *moved, fc, fd, fe)


def solution(mesh):
    placed = (
        P("grp", None, "slab"),
        P("grp", None, "slab"),
        P("grp", None, "slab"),
        P(),
        P("grp", None, "slab"),
        P("grp", "slab", None),
    )
    return jax.shard_map(
        functools.partial(local, mesh.shape["grp"], mesh.shape["slab"]),
        mesh=mesh,
        in_specs=placed,
        out_specs=(P("grp", None, "slab"), P("grp", None, "slab")),
        check_vma=False,
    )
```

```python
import functools
import jax
import jax.numpy as jnp
import numpy as np
from jax import lax
from jax.experimental import pallas as pl
from jax.experimental.pallas import tpu as pltpu
from jax.sharding import PartitionSpec as P

BRICK = 8
F32 = jnp.float32
BF16 = jnp.bfloat16
MESH = pl.DeviceIdType.MESH
VM = pl.BlockSpec(memory_space=pltpu.VMEM)
HB = pl.BlockSpec(memory_space=pltpu.HBM)

NEAR = [(dx, dz) for dx in (-1, 0, 1) for dz in (-2, -1, 0, 1, 2) if (dx, dz) != (0, 0)]


def split3(a):
    hi = a.astype(BF16)
    rest = a - hi.astype(F32)
    mid = rest.astype(BF16)
    lo = (rest - mid.astype(F32)).astype(BF16)
    return hi, mid, lo


def dot3(a, b):
    parts = [jnp.dot(p, b, preferred_element_type=F32) for p in split3(a)]
    return parts[0] + (parts[1] + parts[2])


def iota(shape, dim):
    return lax.broadcasted_iota(jnp.int32, shape, dim)


def exchange_kernel(
    groups, slabs, source_in, occ_in, cls_in, par_in, coarse_in, table_in, fold_in, fc_in, fd_in, fe_in,
    source, tab, fc, fd, fe, msgz, s13, rz, rc, rf, rfx, rsrc, rs13,
    occ, cls, par, coarse, table, fold, msgx, xs13, send_sem, recv_sem, load_sem,
):
    g = lax.axis_index("grp")
    s = lax.axis_index("slab")
    nx, ny, nz = source.shape
    half = nx // 2

    def exists(dx, dz):
        return (g + dx >= 0) & (g + dx < groups) & (s + dz >= 0) & (s + dz < slabs)

    pairs = (
        (source_in, source), (fold_in, fold), (coarse_in, coarse), (occ_in, occ), (cls_in, cls),
        (par_in, par), (table_in, table), (fc_in, fc), (fd_in, fd), (fe_in, fe),
    )
    loads = [pltpu.make_async_copy(a, b, load_sem.at[i]) for i, (a, b) in enumerate(pairs)]
    for load in loads:
        load.start()
    for ref in (rz, rc, rf, rfx, rsrc, rs13):
        ref[...] = jnp.zeros(ref.shape, F32)
    barrier = pltpu.get_barrier_semaphore()
    count = jnp.int32(0)
    for dx, dz in NEAR:
        here = exists(dx, dz)
        count = count + here.astype(jnp.int32)

        @pl.when(here)
        def _():
            pl.semaphore_signal(
                barrier, inc=1, device_id={"grp": g + dx, "slab": s + dz}, device_id_type=MESH
            )

    for load in loads[:7]:
        load.wait()
    for i in range(table.shape[0]):
        tab[i : i + 1, :] = jnp.full((1, 128), table[i], F32)
    lane = iota((8, 128), 1)
    for c in range(4):
        msgz[4 * c : 4 * c + 4, :] = coarse[0, :, 128 * c : 128 * c + 128]
    msgz[16:32, :] = jnp.zeros((16, 128), F32)
    bx = occ.shape[0]
    for i in range(bx):
        msgz[16 + 4 * i : 20 + 4 * i, 0:16] = occ[i].astype(F32)
        msgz[16 + 4 * i : 20 + 4 * i, 16:32] = cls[i].astype(F32)
    msgz[16:32, 32:40] = jnp.broadcast_to(par[0, 0:1, :].astype(F32), (16, 8))
    for t in range(4):
        tile = jnp.zeros((8, 128), F32)
        for j in range(8):
            for yh in range(4):
                off = (j * 4 + yh) * 4
                v = source[t * 8 + j, yh * 8 : yh * 8 + 8, :]
                r = pltpu.roll(v, off, 1) if off else v
                tile = jnp.where(((lane + 2 - off) & 127) < 4, r, tile)
        msgz[32 + 8 * t : 40 + 8 * t, :] = tile
    for m in range(half):
        a = source[2 * m, pl.ds(0, 16, 2), :] + source[2 * m, pl.ds(1, 16, 2), :]
        b = source[2 * m + 1, pl.ds(0, 16, 2), :] + source[2 * m + 1, pl.ds(1, 16, 2), :]
        s13[m] = a + b
    flat = s13[...].reshape(half * 16, 128)
    s13[...] = dot3(flat, fold[...]).reshape(half, 16, 128)
    for t in range(2):
        tile = jnp.zeros((8, 128), F32)
        for j in range(8):
            for yh in range(2):
                off = (j * 2 + yh) * 8
                v = s13[t * 8 + j, yh * 8 : yh * 8 + 8, :]
                low = pltpu.roll(v, (off + 4) % 128, 1)
                high = pltpu.roll(v, (off + 68) % 128, 1)
                tile = jnp.where((lane >= off) & (lane < off + 4), high, tile)
                tile = jnp.where((lane >= off + 4) & (lane < off + 8), low, tile)
        msgz[64 + 8 * t : 72 + 8 * t, :] = tile
    lane16 = iota((16, 128), 1)
    for side in range(2):
        msgx[side, 0:8, :] = msgz[8 * side : 8 * side + 8, :]
        msgx[side, 8:16, :] = msgz[16 + 8 * side : 24 + 8 * side, :]
        msgx[side, 16:24, :] = msgz[32 + 24 * side : 40 + 24 * side, :]
        msgx[side, 24:32, :] = msgz[64 + 8 * side : 72 + 8 * side, :]
        base = (half - 4) * side
        for i in range(2):
            xs13[side, i] = jnp.where(
                lane16 < 64, s13[base + i], pltpu.roll(s13[base + 2 + i], 64, 1)
            )

    pl.semaphore_wait(barrier, count)

    copies = []

    def add(src, dst, dx, dz):
        k = len(copies)
        copies.append((src, dst, dx, dz, k))

    for dz in (-1, 1):
        add(msgz, rz.at[(1 - dz) // 2], 0, dz)
    for dx in (-1, 1):
        side, slot = (dx + 1) // 2, (1 - dx) // 2
        add(source.at[(nx - 2) * side : (nx - 2) * side + 2], rsrc.at[slot], dx, 0)
        add(xs13.at[side], rs13.at[slot], dx, 0)
        add(msgx.at[side, 0:16], rc.at[slot, 1, 0:16], dx, 0)
        for dz in (-1, 1):
            add(msgx.at[side], rc.at[slot, 1 - dz], dx, dz)
        for dz in (-2, 2):
            add(msgx.at[side, 0:8], rfx.at[slot, (2 - dz) // 4], dx, dz)
    for dz in (-2, 2):
        add(msgz.at[0:16], rf.at[(2 - dz) // 4], 0, dz)

    made = []
    for src, dst, dx, dz, k in copies:
        copy = pltpu.make_async_remote_copy(
            src_ref=src, dst_ref=dst, send_sem=send_sem.at[k], recv_sem=recv_sem.at[k],
            device_id={"grp": g + dx, "slab": s + dz}, device_id_type=MESH,
        )
        made.append((copy, dx, dz))
        pl.when(exists(dx, dz))(copy.start)
    for load in loads[7:]:
        load.wait()
    for copy, dx, dz in made:
        pl.when(exists(-dx, -dz))(copy.wait_recv)
    for copy, dx, dz in made:
        pl.when(exists(dx, dz))(copy.wait_send)


def y_sum(v):
    rows = v.shape[0]
    at = iota(v.shape, 0)
    up = jnp.where(at == 0, 0.0, pltpu.roll(v, 1, 0))
    down = jnp.where(at == rows - 1, 0.0, pltpu.roll(v, rows - 1, 0))
    return up + down


def parts_of(v, zs):
    b = 4.0 * v + zs
    a = 4.0 * v + y_sum(v)
    c = 4.0 * b + y_sum(b)
    return c, a + b


def smooth_kernel(
    slab_rows, source, tab, fc, fd, fe, msgz, s13, rz, rc, rf, rfx, rsrc, rs13,
    middle, finest,
    pf, px, qx, pm, qm, occm, occf, v13, wr13, v14, wr14,
):
    s = lax.axis_index("slab")
    nx, ny, nz = source.shape
    half = nx // 2

    def ext(own, low, high):
        lane = iota(own.shape, 1)
        return jnp.where(
            lane < 40, own, jnp.where(lane < 80, pltpu.roll(low, 40, 1), pltpu.roll(high, 80, 1))
        )

    e_low = ext(rc[0, 1, 8:16], rc[0, 0, 8:16], rc[0, 2, 8:16])
    e_own = ext(msgz[16:32], rz[0, 16:32], rz[1, 16:32])
    e_high = ext(rc[1, 1, 8:16], rc[1, 0, 8:16], rc[1, 2, 8:16])
    e_all = jnp.concatenate([e_low, e_own, e_high], axis=0)
    spread = jnp.dot(e_all.astype(BF16), fc[...], preferred_element_type=F32)

    def coefficients(occupied, label):
        weight = jnp.zeros_like(label)
        for i in range(tab.shape[0]):
            value = jnp.concatenate([tab[i : i + 1, :]] * (label.shape[1] // 128), axis=1)
            weight = jnp.where(label == float(i), jnp.broadcast_to(value, label.shape), weight)
        screen = 4.0 * weight
        inverse = occupied / (8.0 / 3.0 + screen * (8.0 / 27.0))
        p = inverse * (1.0 / 9.0)
        return p, p * ((screen - 18.0) * (1.0 / 36.0))

    of, om = spread[:, 0:256], spread[:, 512:640]
    p, q = coefficients(of, spread[:, 256:512])
    pf[...] = p
    for i in range(8):
        for j in range(4):
            for tile in range(2):
                cut = slice(128 * tile, 128 * tile + 128)
                one = slice(4 * i + j, 4 * i + j + 1)
                px[i, tile, 8 * j : 8 * j + 8, :] = jnp.broadcast_to(p[one, cut], (8, 128))
                qx[i, tile, 8 * j : 8 * j + 8, :] = jnp.broadcast_to(q[one, cut], (8, 128))
    p, q = coefficients(om, spread[:, 640:768])
    for i in range(8):
        for value, ref in ((p, pm), (q, qm), (om, occm), (of, occf)):
            rows = [
                jnp.broadcast_to(value[4 * i + j : 4 * i + j + 1], (4, value.shape[1]))
                for j in range(4)
            ]
            ref[i] = jnp.concatenate(rows, axis=0)

    base = ((s - 2) * slab_rows).astype(F32)

    def bricks(ext_rows, blocks, cs):
        cand = jnp.concatenate(blocks, axis=0)
        n_rows, n_cand = cs * 8, 5 * cs * 4
        row = jnp.broadcast_to(ext_rows[0:1], (n_rows, 128))
        kk = iota((n_rows, 128), 0) & 7
        at = jnp.where(kk == 0, 78, jnp.where(kk == 5, 112, 30 + 2 * kk))
        at = jnp.where(kk > 5, 127, at)
        pos = jnp.sum(jnp.where(iota((n_rows, 128), 1) == at, row, 0.0), axis=1, keepdims=True)
        col = iota((n_rows, n_cand), 1)
        r = iota((n_rows, n_cand), 0)
        block = col // (cs * 4)
        c_of = (col // 4) % cs
        place = (block * 4 + col % 4).astype(F32)
        hot = ((c_of == r // 8) & (pos - base == place)).astype(F32).astype(BF16)
        hi, mid, lo = split3(cand)
        return [jnp.dot(hot, part, preferred_element_type=F32) for part in (hi, mid, lo)]

    own = bricks(e_own, [rf[0], rz[0, 0:16], msgz[0:16], rz[1, 0:16], rf[1]], 4)
    sides = [
        bricks(e, [rfx[i, 0], rc[i, 0, 0:8], rc[i, 1, 0:8], rc[i, 2, 0:8], rfx[i, 1]], 2)
        for i, e in ((0, e_low), (1, e_high))
    ]
    keep = (iota((16, 128), 1) // 8) == iota((16, 128), 0)
    total = None
    for part in range(3):
        lines = []
        for rows, cs in ((sides[0][part], 2), (own[part], 4), (sides[1][part], 2)):
            for c in range(cs):
                lines.append(jnp.concatenate(
                    [
                        jnp.where(keep, jnp.broadcast_to(rows[8 * c + k : 8 * c + k + 1], (16, 128)), 0.0)
                        for k in range(6)
                    ], axis=1))
        left = jnp.concatenate(lines, axis=0).astype(BF16)
        term = jnp.dot(left, fd[...], preferred_element_type=F32)
        total = term if total is None else total + term
    for i in range(1, 15):
        line = total[8 * i : 8 * i + 8]
        for a in range(2):
            plane = 2 * i - 2 + a
            v13[0, plane, pl.ds(0, 8, 2), :] = line
            v13[0, plane, pl.ds(1, 8, 2), :] = line
    for plane in range(28):
        brick = min(max((plane - 6) // 4 + 2, 0), 7)
        v13[0, plane] = v13[0, plane] * occm[brick]

    lane16 = iota((16, 128), 1)
    lane8 = iota((8, 128), 1)

    def strip13(low, high, j, own_plane):
        both = jnp.where((lane8 & 7) < 4, low, high)
        rows = []
        for yh in range(2):
            off = (j * 2 + yh) * 8
            to_low = pltpu.roll(both, (124 - off) % 128, 1)
            to_high = pltpu.roll(both, (60 - off) % 128, 1)
            rows.append(jnp.where(
                lane8 < 64, own_plane[8 * yh : 8 * yh + 8],
                jnp.where(lane8 < 96, to_high, to_low)))
        return jnp.concatenate(rows, axis=0)

    for m in range(-4, half + 4):
        if m < 0 or m >= half:
            side, i = (0, m + 4) if m < 0 else (1, m - half)
            own_plane = rs13[side, i % 2]
            if i >= 2:
                own_plane = pltpu.roll(own_plane, 64, 1)
            j = (m if m >= 0 else half + m) % 8
            plane = strip13(rc[side, 0, 24:32], rc[side, 2, 24:32], j, own_plane)
        else:
            t = m // 8
            plane = strip13(rz[0, 64 + 8 * t : 72 + 8 * t], rz[1, 64 + 8 * t : 72 + 8 * t], m % 8, s13[m])
        wr13[m + 4] = plane * (6.0 * pm[m // 4 + 2])

    def strip14(low, high, j):
        both = jnp.where((lane8 & 3) < 2, high, low)
        rows = []
        for yh in range(4):
            off = (j * 4 + yh) * 4
            rows.append(pltpu.roll(both, 128 - off, 1) if off else both)
        return rows

    for x in range(-2, nx + 2):
        if x < 0 or x >= nx:
            side, i = (0, x + 2) if x < 0 else (1, x - nx)
            own_plane = rsrc[side, i]
            j = (x if x >= 0 else nx + x) % 8
            rows = strip14(rc[side, 0, 16:24], rc[side, 2, 16:24], j)
        else:
            t = x // 8
            own_plane = source[x]
            rows = strip14(rz[0, 32 + 8 * t : 40 + 8 * t], rz[1, 32 + 8 * t : 40 + 8 * t], x % 8)
        xb = x // 8 + 2
        for yh in range(4):
            w = 6.0 * pf[4 * xb + yh : 4 * xb + yh + 1, :]
            wr14[x + 2, 8 * yh : 8 * yh + 8, 0:128] = own_plane[8 * yh : 8 * yh + 8] * w[:, 0:128]
            wr14[x + 2, 8 * yh : 8 * yh + 8, 128:256] = rows[yh] * w[:, 128:256]

    for sweep in range(3):
        old, new = sweep % 2, (sweep + 1) % 2
        first, last = sweep - 4, half + 3 - sweep

        def pieces(i):
            v = v13[old, i + 6]
            return parts_of(v, pltpu.roll(v, 1, 1) + pltpu.roll(v, 127, 1))

        c0, e0 = pieces(first - 1)
        c1, e1 = pieces(first)
        for m in range(first, last + 1):
            c2, e2 = pieces(m + 1)
            b = m // 4 + 2
            bx_e = 4.0 * e1 + (e0 + e2)
            bx_c = 4.0 * c1 + (c0 + c2)
            out = v13[old, m + 6] + wr13[m + 4] - pm[b] * (c1 + bx_e) - qm[b] * bx_c
            v13[new, m + 6] = out
            if sweep == 2 and 0 <= m < half:
                middle[m] = out[:, 0:64]
            c0, e0, c1, e1 = c1, e1, c2, e2

    wide = dot3(v13[1, 4 : half + 8].reshape((half + 4) * 16, 128), fe[...])
    for i in range(half + 4):
        m = i - 2
        line = wide[16 * i : 16 * i + 16] * occf[m // 4 + 2]
        for a in range(2):
            for b in range(2):
                v14[0, 2 * i + a, b, pl.ds(0, 16, 2), :] = line[:, 128 * b : 128 * b + 128]
                v14[0, 2 * i + a, b, pl.ds(1, 16, 2), :] = line[:, 128 * b : 128 * b + 128]

    lane32 = iota((ny, 128), 1)
    for sweep in range(3):
        old, new = sweep % 2, (sweep + 1) % 2
        first, last = sweep - 2, nx + 1 - sweep
        tiles = 2 if sweep < 2 else 1

        def pieces(i):
            v0 = v14[old, i, 0]
            v1 = v14[old, i, 1]
            l0, l1 = pltpu.roll(v0, 1, 1), pltpu.roll(v1, 1, 1)
            r0, r1 = pltpu.roll(v0, 127, 1), pltpu.roll(v1, 127, 1)
            z0 = jnp.where(lane32 == 0, l1, l0) + jnp.where(lane32 == 127, r1, r0)
            got = [parts_of(v0, z0)]
            if tiles == 2:
                z1 = jnp.where(lane32 == 0, l0, l1) + jnp.where(lane32 == 127, r0, r1)
                got.append(parts_of(v1, z1))
            return got

        def step(i, carry):
            before, now = carry
            after = pieces(i + 1)
            xb = (i + 12) // 8
            for t in range(tiles):
                cut = slice(128 * t, 128 * t + 128)
                (c0, e0), (c1, e1), (c2, e2) = before[t], now[t], after[t]
                u = c1 + (4.0 * e1 + (e0 + e2))
                w = 4.0 * c1 + (c0 + c2)
                for yh in range(4):
                    r = slice(8 * yh, 8 * yh + 8)
                    p = px[xb, t, r]
                    q = qx[xb, t, r]
                    out = v14[old, i, t, r] + wr14[i - 2, r, cut] - p * u[r] - q * w[r]
                    if sweep == 2:
                        finest[i - 4, r, :] = out
                    else:
                        v14[new, i, t, r] = out
            return now, after

        lax.fori_loop(first + 4, last + 5, step, (pieces(first + 3), pieces(first + 4)))


def constants():
    fc = np.zeros((128, 768), np.float32)
    for j in range(256):
        z = j if j < 192 else j - 256
        if 0 <= z < 128:
            at = z // 8
        elif -16 <= z < 0:
            at = 56 + z // 8
        elif 128 <= z < 144:
            at = 80 + (z - 128) // 8
        else:
            continue
        fc[at, j] = 1
        fc[at + 16, 256 + j] = 1
    for j in range(128):
        z = j if j < 96 else j - 128
        if 0 <= z < 64:
            at = z // 4
        elif -8 <= z < 0:
            at = 56 + z // 4
        elif 64 <= z < 72:
            at = 80 + (z - 64) // 4
        else:
            continue
        fc[at, 512 + j] = 1
        fc[at + 16, 640 + j] = 1
    fd = np.zeros((768, 128), np.float32)
    for k in range(6):
        for l in range(128):
            for b in range(2):
                z = (k - 1) * 16 + 2 * (l % 8) + b
                if -8 <= z < 72:
                    fd[k * 128 + l, z % 128] = 1
    fe = np.zeros((128, 256), np.float32)
    for j in range(256):
        z = j if j < 192 else j - 256
        if -8 <= z < 136:
            fe[(z // 2) % 128, j] = 1
    fold = np.zeros((128, 128), np.float32)
    for z in range(128):
        fold[z, z // 2] = 0.25
    return [jnp.asarray(a, BF16) for a in (fold, fc, fd, fe)]


def local(groups, slabs, source, occupancy, classes, screen_table, parents, coarse):
    nx, ny, nz = source.shape
    half = nx // 2
    fold, fc, fd, fe = constants()
    shape = lambda *dims: jax.ShapeDtypeStruct(dims, F32)
    moved = pl.pallas_call(
        functools.partial(exchange_kernel, groups, slabs),
        out_shape=[
            shape(nx, ny, nz), shape(screen_table.shape[0], 128),
            *(jax.ShapeDtypeStruct(a.shape, BF16) for a in (fc, fd, fe)),
            shape(80, 128), shape(half, 16, 128), shape(2, 80, 128), shape(2, 3, 32, 128),
            shape(2, 16, 128), shape(2, 2, 8, 128), shape(2, 2, ny, nz), shape(2, 2, 16, 128),
        ],
        in_specs=[HB] * 10,
        out_specs=[VM] * 13,
        scratch_shapes=[
            pltpu.VMEM(occupancy.shape, jnp.int32), pltpu.VMEM(classes.shape, jnp.int32),
            pltpu.VMEM(parents.shape, jnp.int32), pltpu.VMEM(coarse.shape, F32),
            pltpu.SMEM(screen_table.shape, F32), pltpu.VMEM(fold.shape, BF16),
            pltpu.VMEM((2, 32, 128), F32),
            pltpu.VMEM((2, 2, 16, 128), F32),
            pltpu.SemaphoreType.DMA((18,)),
            pltpu.SemaphoreType.DMA((18,)),
            pltpu.SemaphoreType.DMA((10,)),
        ],
        compiler_params=pltpu.CompilerParams(
            collective_id=0, has_side_effects=True, vmem_limit_bytes=24 << 20
        ),
        name="exchange",
    )(*(
        pltpu.with_memory_space_constraint(a, pltpu.HBM)
        for a in (source, occupancy, classes, parents, coarse, screen_table, fold, fc, fd, fe)
    ))
    return pl.pallas_call(
        functools.partial(smooth_kernel, coarse.shape[1]),
        out_shape=[shape(half, ny // 2, nz // 2), shape(nx, ny, nz)],
        in_specs=[VM] * 13,
        out_specs=[VM] * 2,
        scratch_shapes=[
            pltpu.VMEM((32, 256), F32),
            pltpu.VMEM((8, 2, ny, 128), F32), pltpu.VMEM((8, 2, ny, 128), F32),
            pltpu.VMEM((8, 16, 128), F32), pltpu.VMEM((8, 16, 128), F32),
            pltpu.VMEM((8, 16, 128), F32), pltpu.VMEM((8, 16, 256), F32),
            pltpu.VMEM((2, half + 12, 16, 128), F32),
            pltpu.VMEM((half + 8, 16, 128), F32),
            pltpu.VMEM((2, nx + 8, 2, ny, 128), F32),
            pltpu.VMEM((nx + 4, ny, 256), F32),
        ],
        compiler_params=pltpu.CompilerParams(vmem_limit_bytes=32 << 20),
        name="smooth",
    )(*moved)


def solution(mesh):
    placed = (
        P("grp", None, "slab"),
        P("grp", None, "slab"),
        P("grp", None, "slab"),
        P(),
        P("grp", None, "slab"),
        P("grp", "slab", None),
    )
    return jax.shard_map(
        functools.partial(local, mesh.shape["grp"], mesh.shape["slab"]),
        mesh=mesh,
        in_specs=placed,
        out_specs=(P("grp", None, "slab"), P("grp", None, "slab")),
        check_vma=False,
    )
```

```python
import functools
import jax
import jax.numpy as jnp
import numpy as np
from jax import lax
from jax.experimental import pallas as pl
from jax.experimental.pallas import tpu as pltpu
from jax.sharding import PartitionSpec as P

BRICK = 8
F32 = jnp.float32
BF16 = jnp.bfloat16
MESH = pl.DeviceIdType.MESH
VM = pl.BlockSpec(memory_space=pltpu.VMEM)
HB = pl.BlockSpec(memory_space=pltpu.HBM)

NEAR = [(dx, dz) for dx in (-1, 0, 1) for dz in (-2, -1, 0, 1, 2) if (dx, dz) != (0, 0)]


def split3(a):
    hi = a.astype(BF16)
    rest = a - hi.astype(F32)
    mid = rest.astype(BF16)
    lo = (rest - mid.astype(F32)).astype(BF16)
    return hi, mid, lo


def dot3(a, b):
    parts = [jnp.dot(p, b, preferred_element_type=F32) for p in split3(a)]
    return parts[0] + (parts[1] + parts[2])


def iota(shape, dim):
    return lax.broadcasted_iota(jnp.int32, shape, dim)


def exchange_kernel(
    groups, slabs, source_in, occ_in, cls_in, par_in, coarse_in, table_in, fold_in, fc_in, fd_in, fe_in,
    source, tab, fc, fd, fe, msgz, s13, rz, rc, rf, rfx, rsrc, rs13,
    occ, cls, par, coarse, table, fold, msgx, xs13, send_sem, recv_sem, load_sem,
):
    g = lax.axis_index("grp")
    s = lax.axis_index("slab")
    nx, ny, nz = source.shape
    half = nx // 2

    def exists(dx, dz):
        return (g + dx >= 0) & (g + dx < groups) & (s + dz >= 0) & (s + dz < slabs)

    pairs = (
        (source_in, source), (fold_in, fold), (coarse_in, coarse), (occ_in, occ), (cls_in, cls),
        (par_in, par), (table_in, table), (fc_in, fc), (fd_in, fd), (fe_in, fe),
    )
    loads = [pltpu.make_async_copy(a, b, load_sem.at[i]) for i, (a, b) in enumerate(pairs)]
    for load in loads:
        load.start()
    for ref in (rz, rc, rf, rfx, rsrc, rs13):
        ref[...] = jnp.zeros(ref.shape, F32)
    barrier = pltpu.get_barrier_semaphore()
    count = jnp.int32(0)
    for dx, dz in NEAR:
        here = exists(dx, dz)
        count = count + here.astype(jnp.int32)

        @pl.when(here)
        def _():
            pl.semaphore_signal(
                barrier, inc=1, device_id={"grp": g + dx, "slab": s + dz}, device_id_type=MESH
            )

    for load in loads[:7]:
        load.wait()
    for i in range(table.shape[0]):
        tab[i : i + 1, :] = jnp.full((1, 128), table[i], F32)
    lane = iota((8, 128), 1)
    for c in range(4):
        msgz[4 * c : 4 * c + 4, :] = coarse[0, :, 128 * c : 128 * c + 128]
    msgz[16:32, :] = jnp.zeros((16, 128), F32)
    bx = occ.shape[0]
    for i in range(bx):
        msgz[16 + 4 * i : 20 + 4 * i, 0:16] = occ[i].astype(F32)
        msgz[16 + 4 * i : 20 + 4 * i, 16:32] = cls[i].astype(F32)
    msgz[16:32, 32:40] = jnp.broadcast_to(par[0, 0:1, :].astype(F32), (16, 8))
    for t in range(4):
        tile = jnp.zeros((8, 128), F32)
        for j in range(8):
            for yh in range(4):
                off = (j * 4 + yh) * 4
                v = source[t * 8 + j, yh * 8 : yh * 8 + 8, :]
                r = pltpu.roll(v, off, 1) if off else v
                tile = jnp.where(((lane + 2 - off) & 127) < 4, r, tile)
        msgz[32 + 8 * t : 40 + 8 * t, :] = tile
    for m in range(half):
        a = source[2 * m, pl.ds(0, 16, 2), :] + source[2 * m, pl.ds(1, 16, 2), :]
        b = source[2 * m + 1, pl.ds(0, 16, 2), :] + source[2 * m + 1, pl.ds(1, 16, 2), :]
        s13[m] = a + b
    flat = s13[...].reshape(half * 16, 128)
    s13[...] = dot3(flat, fold[...]).reshape(half, 16, 128)
    for t in range(2):
        tile = jnp.zeros((8, 128), F32)
        for j in range(8):
            for yh in range(2):
                off = (j * 2 + yh) * 8
                v = s13[t * 8 + j, yh * 8 : yh * 8 + 8, :]
                low = pltpu.roll(v, (off + 4) % 128, 1)
                high = pltpu.roll(v, (off + 68) % 128, 1)
                tile = jnp.where((lane >= off) & (lane < off + 4), high, tile)
                tile = jnp.where((lane >= off + 4) & (lane < off + 8), low, tile)
        msgz[64 + 8 * t : 72 + 8 * t, :] = tile
    lane16 = iota((16, 128), 1)
    for side in range(2):
        msgx[side, 0:8, :] = msgz[8 * side : 8 * side + 8, :]
        msgx[side, 8:16, :] = msgz[16 + 8 * side : 24 + 8 * side, :]
        msgx[side, 16:24, :] = msgz[32 + 24 * side : 40 + 24 * side, :]
        msgx[side, 24:32, :] = msgz[64 + 8 * side : 72 + 8 * side, :]
        base = (half - 4) * side
        for i in range(2):
            xs13[side, i] = jnp.where(
                lane16 < 64, s13[base + i], pltpu.roll(s13[base + 2 + i], 64, 1)
            )

    pl.semaphore_wait(barrier, count)

    copies = []

    def add(src, dst, dx, dz):
        k = len(copies)
        copies.append((src, dst, dx, dz, k))

    for dz in (-1, 1):
        add(msgz, rz.at[(1 - dz) // 2], 0, dz)
    for dx in (-1, 1):
        side, slot = (dx + 1) // 2, (1 - dx) // 2
        add(source.at[(nx - 2) * side : (nx - 2) * side + 2], rsrc.at[slot], dx, 0)
        add(xs13.at[side], rs13.at[slot], dx, 0)
        add(msgx.at[side, 0:16], rc.at[slot, 1, 0:16], dx, 0)
        for dz in (-1, 1):
            add(msgx.at[side], rc.at[slot, 1 - dz], dx, dz)
        for dz in (-2, 2):
            add(msgx.at[side, 0:8], rfx.at[slot, (2 - dz) // 4], dx, dz)
    for dz in (-2, 2):
        add(msgz.at[0:16], rf.at[(2 - dz) // 4], 0, dz)

    made = []
    for src, dst, dx, dz, k in copies:
        copy = pltpu.make_async_remote_copy(
            src_ref=src, dst_ref=dst, send_sem=send_sem.at[k], recv_sem=recv_sem.at[k],
            device_id={"grp": g + dx, "slab": s + dz}, device_id_type=MESH,
        )
        made.append((copy, dx, dz))
        pl.when(exists(dx, dz))(copy.start)
    for load in loads[7:]:
        load.wait()
    for copy, dx, dz in made:
        pl.when(exists(-dx, -dz))(copy.wait_recv)
    for copy, dx, dz in made:
        pl.when(exists(dx, dz))(copy.wait_send)


def y_sum(v):
    rows = v.shape[0]
    at = iota(v.shape, 0)
    up = jnp.where(at == 0, 0.0, pltpu.roll(v, 1, 0))
    down = jnp.where(at == rows - 1, 0.0, pltpu.roll(v, rows - 1, 0))
    return up + down


def parts_of(v, zs):
    b = 4.0 * v + zs
    a = 4.0 * v + y_sum(v)
    c = 4.0 * b + y_sum(b)
    return c, a + b


def smooth_kernel(
    slab_rows, source, tab, fc, fd, fe, msgz, s13, rz, rc, rf, rfx, rsrc, rs13,
    middle, finest,
    pf, px, qx, pm, qm, occm, occf, v13, wr13, v14, wr14,
):
    s = lax.axis_index("slab")
    nx, ny, nz = source.shape
    half = nx // 2

    def ext(own, low, high):
        lane = iota(own.shape, 1)
        return jnp.where(
            lane < 40, own, jnp.where(lane < 80, pltpu.roll(low, 40, 1), pltpu.roll(high, 80, 1))
        )

    e_low = ext(rc[0, 1, 8:16], rc[0, 0, 8:16], rc[0, 2, 8:16])
    e_own = ext(msgz[16:32], rz[0, 16:32], rz[1, 16:32])
    e_high = ext(rc[1, 1, 8:16], rc[1, 0, 8:16], rc[1, 2, 8:16])
    e_all = jnp.concatenate([e_low, e_own, e_high], axis=0)
    spread = jnp.dot(e_all.astype(BF16), fc[...], preferred_element_type=F32)

    def coefficients(occupied, label):
        weight = jnp.zeros_like(label)
        for i in range(tab.shape[0]):
            value = jnp.concatenate([tab[i : i + 1, :]] * (label.shape[1] // 128), axis=1)
            weight = jnp.where(label == float(i), jnp.broadcast_to(value, label.shape), weight)
        screen = 4.0 * weight
        inverse = occupied / (8.0 / 3.0 + screen * (8.0 / 27.0))
        p = inverse * (1.0 / 9.0)
        return p, p * ((screen - 18.0) * (1.0 / 36.0))

    of, om = spread[:, 0:256], spread[:, 512:640]
    p, q = coefficients(of, spread[:, 256:512])
    pf[...] = p
    for i in range(8):
        for j in range(4):
            for tile in range(2):
                cut = slice(128 * tile, 128 * tile + 128)
                one = slice(4 * i + j, 4 * i + j + 1)
                px[i, tile, 8 * j : 8 * j + 8, :] = jnp.broadcast_to(p[one, cut], (8, 128))
                qx[i, tile, 8 * j : 8 * j + 8, :] = jnp.broadcast_to(q[one, cut], (8, 128))
    p, q = coefficients(om, spread[:, 640:768])
    for i in range(8):
        for value, ref in ((p, pm), (q, qm), (om, occm), (of, occf)):
            rows = [
                jnp.broadcast_to(value[4 * i + j : 4 * i + j + 1], (4, value.shape[1]))
                for j in range(4)
            ]
            ref[i] = jnp.concatenate(rows, axis=0)

    base = ((s - 2) * slab_rows).astype(F32)

    def bricks(ext_rows, blocks, cs):
        cand = jnp.concatenate(blocks, axis=0)
        n_rows, n_cand = cs * 8, 5 * cs * 4
        row = jnp.broadcast_to(ext_rows[0:1], (n_rows, 128))
        kk = iota((n_rows, 128), 0) & 7
        at = jnp.where(kk == 0, 78, jnp.where(kk == 5, 112, 30 + 2 * kk))
        at = jnp.where(kk > 5, 127, at)
        pos = jnp.sum(jnp.where(iota((n_rows, 128), 1) == at, row, 0.0), axis=1, keepdims=True)
        col = iota((n_rows, n_cand), 1)
        r = iota((n_rows, n_cand), 0)
        block = col // (cs * 4)
        c_of = (col // 4) % cs
        place = (block * 4 + col % 4).astype(F32)
        hot = ((c_of == r // 8) & (pos - base == place)).astype(F32).astype(BF16)
        hi, mid, lo = split3(cand)
        return [jnp.dot(hot, part, preferred_element_type=F32) for part in (hi, mid, lo)]

    own = bricks(e_own, [rf[0], rz[0, 0:16], msgz[0:16], rz[1, 0:16], rf[1]], 4)
    sides = [
        bricks(e, [rfx[i, 0], rc[i, 0, 0:8], rc[i, 1, 0:8], rc[i, 2, 0:8], rfx[i, 1]], 2)
        for i, e in ((0, e_low), (1, e_high))
    ]
    keep = (iota((16, 128), 1) // 8) == iota((16, 128), 0)
    total = None
    for part in range(3):
        lines = []
        for rows, cs in ((sides[0][part], 2), (own[part], 4), (sides[1][part], 2)):
            for c in range(cs):
                lines.append(jnp.concatenate(
                    [
                        jnp.where(keep, jnp.broadcast_to(rows[8 * c + k : 8 * c + k + 1], (16, 128)), 0.0)
                        for k in range(6)
                    ], axis=1))
        left = jnp.concatenate(lines, axis=0).astype(BF16)
        term = jnp.dot(left, fd[...], preferred_element_type=F32)
        total = term if total is None else total + term
    for i in range(1, 15):
        line = total[8 * i : 8 * i + 8]
        for a in range(2):
            plane = 2 * i - 2 + a
            v13[0, plane, pl.ds(0, 8, 2), :] = line
            v13[0, plane, pl.ds(1, 8, 2), :] = line
    for plane in range(28):
        brick = min(max((plane - 6) // 4 + 2, 0), 7)
        v13[0, plane] = v13[0, plane] * occm[brick]

    lane16 = iota((16, 128), 1)
    lane8 = iota((8, 128), 1)

    def strip13(low, high, j, own_plane):
        both = jnp.where((lane8 & 7) < 4, low, high)
        rows = []
        for yh in range(2):
            off = (j * 2 + yh) * 8
            to_low = pltpu.roll(both, (124 - off) % 128, 1)
            to_high = pltpu.roll(both, (60 - off) % 128, 1)
            rows.append(jnp.where(
                lane8 < 64, own_plane[8 * yh : 8 * yh + 8],
                jnp.where(lane8 < 96, to_high, to_low)))
        return jnp.concatenate(rows, axis=0)

    for m in range(-4, half + 4):
        if m < 0 or m >= half:
            side, i = (0, m + 4) if m < 0 else (1, m - half)
            own_plane = rs13[side, i % 2]
            if i >= 2:
                own_plane = pltpu.roll(own_plane, 64, 1)
            j = (m if m >= 0 else half + m) % 8
            plane = strip13(rc[side, 0, 24:32], rc[side, 2, 24:32], j, own_plane)
        else:
            t = m // 8
            plane = strip13(rz[0, 64 + 8 * t : 72 + 8 * t], rz[1, 64 + 8 * t : 72 + 8 * t], m % 8, s13[m])
        wr13[m + 4] = plane * (6.0 * pm[m // 4 + 2])

    def strip14(low, high, j):
        both = jnp.where((lane8 & 3) < 2, high, low)
        rows = []
        for yh in range(4):
            off = (j * 4 + yh) * 4
            rows.append(pltpu.roll(both, 128 - off, 1) if off else both)
        return rows

    for x in range(-2, nx + 2):
        if x < 0 or x >= nx:
            side, i = (0, x + 2) if x < 0 else (1, x - nx)
            own_plane = rsrc[side, i]
            j = (x if x >= 0 else nx + x) % 8
            rows = strip14(rc[side, 0, 16:24], rc[side, 2, 16:24], j)
        else:
            t = x // 8
            own_plane = source[x]
            rows = strip14(rz[0, 32 + 8 * t : 40 + 8 * t], rz[1, 32 + 8 * t : 40 + 8 * t], x % 8)
        xb = x // 8 + 2
        for yh in range(4):
            w = 6.0 * pf[4 * xb + yh : 4 * xb + yh + 1, :]
            wr14[x + 2, 8 * yh : 8 * yh + 8, 0:128] = own_plane[8 * yh : 8 * yh + 8] * w[:, 0:128]
            wr14[x + 2, 8 * yh : 8 * yh + 8, 128:256] = rows[yh] * w[:, 128:256]

    for sweep in range(3):
        old, new = sweep % 2, (sweep + 1) % 2
        first, last = sweep - 4, half + 3 - sweep

        def pieces(i):
            v = v13[old, i + 6]
            return parts_of(v, pltpu.roll(v, 1, 1) + pltpu.roll(v, 127, 1))

        c0, e0 = pieces(first - 1)
        c1, e1 = pieces(first)
        for m in range(first, last + 1):
            c2, e2 = pieces(m + 1)
            b = m // 4 + 2
            bx_e = 4.0 * e1 + (e0 + e2)
            bx_c = 4.0 * c1 + (c0 + c2)
            out = v13[old, m + 6] + wr13[m + 4] - pm[b] * (c1 + bx_e) - qm[b] * bx_c
            v13[new, m + 6] = out
            if sweep == 2 and 0 <= m < half:
                middle[m] = out[:, 0:64]
            c0, e0, c1, e1 = c1, e1, c2, e2

    wide = dot3(v13[1, 4 : half + 8].reshape((half + 4) * 16, 128), fe[...])
    for i in range(half + 4):
        m = i - 2
        line = wide[16 * i : 16 * i + 16] * occf[m // 4 + 2]
        for a in range(2):
            for b in range(2):
                v14[0, 2 * i + a, b, pl.ds(0, 16, 2), :] = line[:, 128 * b : 128 * b + 128]
                v14[0, 2 * i + a, b, pl.ds(1, 16, 2), :] = line[:, 128 * b : 128 * b + 128]

    lane32 = iota((ny, 128), 1)
    for sweep in range(3):
        old, new = sweep % 2, (sweep + 1) % 2
        first, last = sweep - 2, nx + 1 - sweep
        tiles = 2 if sweep < 2 else 1

        def pieces(i):
            v0 = v14[old, i, 0]
            v1 = v14[old, i, 1]
            l0, l1 = pltpu.roll(v0, 1, 1), pltpu.roll(v1, 1, 1)
            r0, r1 = pltpu.roll(v0, 127, 1), pltpu.roll(v1, 127, 1)
            z0 = jnp.where(lane32 == 0, l1, l0) + jnp.where(lane32 == 127, r1, r0)
            got = [parts_of(v0, z0)]
            if tiles == 2:
                z1 = jnp.where(lane32 == 0, l0, l1) + jnp.where(lane32 == 127, r0, r1)
                got.append(parts_of(v1, z1))
            return got

        def step(i, carry):
            before, now = carry
            after = pieces(i + 1)
            xb = (i + 12) // 8
            for t in range(tiles):
                cut = slice(128 * t, 128 * t + 128)
                (c0, e0), (c1, e1), (c2, e2) = before[t], now[t], after[t]
                u = c1 + (4.0 * e1 + (e0 + e2))
                w = 4.0 * c1 + (c0 + c2)
                for yh in range(4):
                    r = slice(8 * yh, 8 * yh + 8)
                    p = px[xb, t, r]
                    q = qx[xb, t, r]
                    out = v14[old, i, t, r] + wr14[i - 2, r, cut] - p * u[r] - q * w[r]
                    if sweep == 2:
                        finest[i - 4, r, :] = out
                    else:
                        v14[new, i, t, r] = out
            return now, after

        lax.fori_loop(first + 4, last + 5, step, (pieces(first + 3), pieces(first + 4)), unroll=True)


def constants():
    fc = np.zeros((128, 768), np.float32)
    for j in range(256):
        z = j if j < 192 else j - 256
        if 0 <= z < 128:
            at = z // 8
        elif -16 <= z < 0:
            at = 56 + z // 8
        elif 128 <= z < 144:
            at = 80 + (z - 128) // 8
        else:
            continue
        fc[at, j] = 1
        fc[at + 16, 256 + j] = 1
    for j in range(128):
        z = j if j < 96 else j - 128
        if 0 <= z < 64:
            at = z // 4
        elif -8 <= z < 0:
            at = 56 + z // 4
        elif 64 <= z < 72:
            at = 80 + (z - 64) // 4
        else:
            continue
        fc[at, 512 + j] = 1
        fc[at + 16, 640 + j] = 1
    fd = np.zeros((768, 128), np.float32)
    for k in range(6):
        for l in range(128):
            for b in range(2):
                z = (k - 1) * 16 + 2 * (l % 8) + b
                if -8 <= z < 72:
                    fd[k * 128 + l, z % 128] = 1
    fe = np.zeros((128, 256), np.float32)
    for j in range(256):
        z = j if j < 192 else j - 256
        if -8 <= z < 136:
            fe[(z // 2) % 128, j] = 1
    fold = np.zeros((128, 128), np.float32)
    for z in range(128):
        fold[z, z // 2] = 0.25
    return [jnp.asarray(a, BF16) for a in (fold, fc, fd, fe)]


def local(groups, slabs, source, occupancy, classes, screen_table, parents, coarse):
    nx, ny, nz = source.shape
    half = nx // 2
    fold, fc, fd, fe = constants()
    shape = lambda *dims: jax.ShapeDtypeStruct(dims, F32)
    moved = pl.pallas_call(
        functools.partial(exchange_kernel, groups, slabs),
        out_shape=[
            shape(nx, ny, nz), shape(screen_table.shape[0], 128),
            *(jax.ShapeDtypeStruct(a.shape, BF16) for a in (fc, fd, fe)),
            shape(80, 128), shape(half, 16, 128), shape(2, 80, 128), shape(2, 3, 32, 128),
            shape(2, 16, 128), shape(2, 2, 8, 128), shape(2, 2, ny, nz), shape(2, 2, 16, 128),
        ],
        in_specs=[HB] * 10,
        out_specs=[VM] * 13,
        scratch_shapes=[
            pltpu.VMEM(occupancy.shape, jnp.int32), pltpu.VMEM(classes.shape, jnp.int32),
            pltpu.VMEM(parents.shape, jnp.int32), pltpu.VMEM(coarse.shape, F32),
            pltpu.SMEM(screen_table.shape, F32), pltpu.VMEM(fold.shape, BF16),
            pltpu.VMEM((2, 32, 128), F32),
            pltpu.VMEM((2, 2, 16, 128), F32),
            pltpu.SemaphoreType.DMA((18,)),
            pltpu.SemaphoreType.DMA((18,)),
            pltpu.SemaphoreType.DMA((10,)),
        ],
        compiler_params=pltpu.CompilerParams(
            collective_id=0, has_side_effects=True, vmem_limit_bytes=24 << 20
        ),
        name="exchange",
    )(*(
        pltpu.with_memory_space_constraint(a, pltpu.HBM)
        for a in (source, occupancy, classes, parents, coarse, screen_table, fold, fc, fd, fe)
    ))
    return pl.pallas_call(
        functools.partial(smooth_kernel, coarse.shape[1]),
        out_shape=[shape(half, ny // 2, nz // 2), shape(nx, ny, nz)],
        in_specs=[VM] * 13,
        out_specs=[VM] * 2,
        scratch_shapes=[
            pltpu.VMEM((32, 256), F32),
            pltpu.VMEM((8, 2, ny, 128), F32), pltpu.VMEM((8, 2, ny, 128), F32),
            pltpu.VMEM((8, 16, 128), F32), pltpu.VMEM((8, 16, 128), F32),
            pltpu.VMEM((8, 16, 128), F32), pltpu.VMEM((8, 16, 256), F32),
            pltpu.VMEM((2, half + 12, 16, 128), F32),
            pltpu.VMEM((half + 8, 16, 128), F32),
            pltpu.VMEM((2, nx + 8, 2, ny, 128), F32),
            pltpu.VMEM((nx + 4, ny, 256), F32),
        ],
        compiler_params=pltpu.CompilerParams(vmem_limit_bytes=32 << 20),
        name="smooth",
    )(*moved)


def solution(mesh):
    placed = (
        P("grp", None, "slab"),
        P("grp", None, "slab"),
        P("grp", None, "slab"),
        P(),
        P("grp", None, "slab"),
        P("grp", "slab", None),
    )
    return jax.shard_map(
        functools.partial(local, mesh.shape["grp"], mesh.shape["slab"]),
        mesh=mesh,
        in_specs=placed,
        out_specs=(P("grp", None, "slab"), P("grp", None, "slab")),
        check_vma=False,
    )
```
